512 devices in a mesh: ctx: 64 (over y_hi, z, core), head: 8 (over y_lo, x).
Axes of the slice: x: 4, y: 4 (y_hi: 2, y_lo: 2; y = y_hi * 2 + y_lo), z: 16, core: 2. Of those that a mesh axis runs over, the one named last changes fastest.
Arguments:
- queries: bfloat16 [512, 8192], P(('ctx', 'head')), may hold values from -120 to 120
- out_grad: bfloat16 [512, 8192], P(('ctx', 'head')), may hold values from -6 to 6
- resp_keys: bfloat16 [512, 1024], P('ctx', 'head'), may hold values from -6 to 6
- resp_values: bfloat16 [512, 1024], P('ctx', 'head'), may hold values from -6 to 6
- prompt_keys: bfloat16 [49152, 1024], P('ctx', 'head'), may hold values from -6 to 6
- prompt_values: bfloat16 [49152, 1024], P('ctx', 'head'), may hold values from -6 to 6
- resp_lengths: int32 [16], replicated, may hold values from 1 to 32, 256 in all
- resp_order: int32 [16], replicated, may hold values from 0 to 15, each once
Outputs:
- query_grad: bfloat16 [512, 8192], P(('ctx', 'head'))
- prompt_key_grad: bfloat16 [49152, 1024], P('ctx', 'head')
- prompt_value_grad: bfloat16 [49152, 1024], P('ctx', 'head')
- resp_key_grad: bfloat16 [512, 1024], P('ctx', 'head')
- resp_value_grad: bfloat16 [512, 1024], P('ctx', 'head')
The draws below stay inside these ranges and needn't reach their ends.
Inputs may be any that keep to these rules, and one draw needn't show every extreme that they name: `resp_lengths`: each response has 1 to 32 tokens, 256 in all, and one has exactly 32. `resp_order`: each response stands in exactly one slot.
All inputs are finite; a program needn't handle non-finite values.
Results may differ from the reference program's by a relative error of at most 0.017.
Values may be sent and summed in bfloat16 or wider, within the bound.
No kernel may reach another device: no remote copies, remote signals or barrier semaphores. Data moves between devices by JAX's collectives and lax.ppermute only.
A program may use at most 64 MiB of HBM per device.

```python
import math
import jax
import jax.numpy as jnp
import numpy as np
from jax import lax

QH = 64
KVH = 8
HD = 128
NRESP = 16
PROMPT = 49152
RESP = 512
MAXLEN = 32
LIVE = 256


def anchor_rows(key):
    base = jax.random.truncated_normal(jax.random.fold_in(key, 100), -6.0, 6.0, (PROMPT, KVH * HD), jnp.float32)
    return base


def draw_prompt_keys(key, part):
    base = anchor_rows(key)
    return base.astype(jnp.bfloat16)


def draw_queries(key, part):
    key = jax.random.fold_in(key, 2)
    result = jax.random.truncated_normal(key, -6.0, 6.0, (RESP, QH * HD), jnp.float32)
    return result.astype(jnp.bfloat16)


def block_levels(own_key, extent, split, low, top_value):
    def one(position, parts):
        draws = jax.random.uniform(jax.random.fold_in(jax.random.fold_in(own_key, 6), position), (parts,), jnp.float32, low / len(split), top_value / len(split))
        return jnp.repeat(jnp.exp(draws), extent[position] // parts).reshape((-1,) + (1,) * (len(extent) - position - 1))

    loudness = one(*split[0])
    for cut in split[1:]:
        loudness = loudness * one(*cut)
    return loudness


def length_profile(number_of, total, bound, skew):
    portions = [(1 << 20) // math.isqrt(rank ** skew) + 1 for rank in range(2, number_of + 1)]
    spare, counts = total - bound - (number_of - 1), [1] * (number_of - 1)
    while spare > 0:
        movable = [i for i in range(number_of - 1) if counts[i] < bound]
        mass, left = sum([portions[i] for i in movable]), spare
        for i in movable:
            addition = min(bound - counts[i], max(1, left * portions[i] // mass), spare)
            counts[i] = counts[i] + addition
            spare = spare - addition
    return np.array([bound] + counts)


def uneven_parts(stream_key, count, total, bound, skew):
    if count == 2:
        one = jax.random.randint(stream_key, (), max(1, total - bound), min(bound, total - 1) + 1)
        return jnp.stack([one, total - one])
    tallies = jnp.asarray(length_profile(count, total, bound, skew), jnp.int32)
    couples = (count - 1) // 2
    giver, taker = tallies[1:1 + 2 * couples:2], tallies[2:2 + 2 * couples:2]
    margin = jnp.minimum(giver - 1, bound - taker)
    moved = jax.random.randint(jax.random.fold_in(stream_key, 1), (couples,), 0, 1 << 20) % (margin + 1)
    tallies = tallies.at[1:1 + 2 * couples:2].set(giver - moved).at[2:2 + 2 * couples:2].set(taker + moved)
    return tallies[jax.random.permutation(jax.random.fold_in(stream_key, 2), count)]


def scatter_about(key, shape, deviation, reach, shards=(), kind=jnp.bfloat16):
    drawn = jax.random.normal(key, shape, jnp.float32) * deviation
    if len(shards) > 0:
        drawn = block_levels(key, shape, shards, -0.22, 0.18) * drawn
    return jnp.clip(drawn, min=-reach, max=reach).astype(kind)


def setup_inputs(seed: int = 0) -> dict:
    streams_of = jax.random.split(jax.random.key(seed), 9)
    queries = draw_queries(jax.random.fold_in(streams_of[8], 71), 0)
    out_grad = scatter_about(streams_of[1], (RESP, QH * HD), 1.0, 6.0, ((0, 512),))
    resp_keys = scatter_about(streams_of[2], (RESP, KVH * HD), 1.0, 6.0, ((0, 64), (1, 8)))
    resp_values = scatter_about(streams_of[3], (RESP, KVH * HD), 1.0, 6.0, ((0, 64), (1, 8)))
    prompt_keys = draw_prompt_keys(jax.random.fold_in(streams_of[8], 71), 0)
    prompt_values = scatter_about(streams_of[5], (PROMPT, KVH * HD), 1.0, 6.0, ((0, 64), (1, 8)))
    resp_lengths = uneven_parts(streams_of[6], NRESP, LIVE, MAXLEN, 2).astype(jnp.int32)
    resp_order = jax.random.permutation(streams_of[7], NRESP).astype(jnp.int32)
    return {"queries": queries, "out_grad": out_grad, "resp_keys": resp_keys, "resp_values": resp_values, "prompt_keys": prompt_keys, "prompt_values": prompt_values, "resp_lengths": resp_lengths, "resp_order": resp_order}


def reference(queries, out_grad, resp_keys, resp_values, prompt_keys, prompt_values, resp_lengths, resp_order):
    total_rows = queries.shape[0]
    group = QH // KVH
    scale = 1.0 / math.sqrt(HD)
    rows = jnp.arange(total_rows, dtype=jnp.int32)
    slot = rows // MAXLEN
    offset = rows % MAXLEN
    slot_len = resp_lengths[resp_order]
    live = offset < slot_len[slot]
    grads = jnp.where(live[:, None], out_grad, jnp.zeros_like(out_grad))
    own = (slot[:, None] == slot[None, :]) & (offset[None, :] <= offset[:, None])
    visible = jnp.concatenate([jnp.ones((total_rows, PROMPT), bool), own], axis=1)
    keys = jnp.concatenate([prompt_keys, resp_keys], axis=0)
    values = jnp.concatenate([prompt_values, resp_values], axis=0)

    def one_group(index):
        key_g = lax.dynamic_slice_in_dim(keys, index * HD, HD, 1)
        value_g = lax.dynamic_slice_in_dim(values, index * HD, HD, 1)

        def one_head(carry, inner):
            key_grad, value_grad = carry
            head = index * group + inner
            q_head = lax.dynamic_slice_in_dim(queries, head * HD, HD, 1)
            g_head = lax.dynamic_slice_in_dim(grads, head * HD, HD, 1)
            logits = jnp.dot(q_head, key_g.T, preferred_element_type=jnp.float32) * scale
            logits = jnp.where(visible, logits, -1e+30)
            prob = jax.nn.softmax(logits, axis=-1)
            dprob = jnp.dot(g_head, value_g.T, preferred_element_type=jnp.float32)
            delta = lax.optimization_barrier(jnp.sum(prob * dprob, axis=-1, keepdims=True))
            dscore = (prob * (dprob - delta)).astype(jnp.bfloat16)
            q_grad = jnp.dot(dscore, key_g, preferred_element_type=jnp.float32) * scale
            key_grad = key_grad + jnp.dot(dscore.T, q_head, preferred_element_type=jnp.float32) * scale
            value_grad = value_grad + jnp.dot(prob.astype(jnp.bfloat16).T, g_head, preferred_element_type=jnp.float32)
            return ((key_grad, value_grad), q_grad)
        start = jnp.zeros((PROMPT + total_rows, HD), jnp.float32)
        (key_grad, value_grad), q_grads = lax.scan(one_head, (start, start), jnp.arange(group, dtype=jnp.int32))
        return (key_grad, value_grad, q_grads)
    key_grads, value_grads, q_grads = lax.map(one_group, jnp.arange(KVH, dtype=jnp.int32))
    query_grad = q_grads.transpose(2, 0, 1, 3).reshape(total_rows, QH * HD).astype(jnp.bfloat16)
    key_all = key_grads.transpose(1, 0, 2).reshape(PROMPT + total_rows, KVH * HD).astype(jnp.bfloat16)
    value_all = value_grads.transpose(1, 0, 2).reshape(PROMPT + total_rows, KVH * HD).astype(jnp.bfloat16)
    return (query_grad, key_all[:PROMPT], value_all[:PROMPT], key_all[PROMPT:], value_all[PROMPT:])
```

```python
import functools
import math

import jax
import jax.numpy as jnp
from jax import lax
from jax.experimental import pallas as pl
from jax.experimental.pallas import tpu as pltpu
from jax.sharding import Mesh
from jax.sharding import PartitionSpec as P

QH = 64
KVH = 8
HD = 128
NRESP = 16
GROUP = QH // KVH
SLOT = 32
NZ = 16
ROWS = 8
BLOCK = ROWS * GROUP
CLASS = NZ * BLOCK
CHUNK = 256
CHUNKS = CLASS // CHUNK
PROMPT_DEV = 768
SHARDS = 4
KEYS = 384
SCALE = 1.0 / math.sqrt(HD)
SCALE2 = SCALE * math.log2(math.e)
F32 = jnp.float32
BF16 = jnp.bfloat16


def nt(a, b):
    return lax.dot_general(a, b, (((1,), (1,)), ((), ())), preferred_element_type=F32)


def nn(a, b):
    return jnp.dot(a, b, preferred_element_type=F32)


def live_rows(lengths_ref, order_ref, z):
    yh, c = lax.axis_index("yh"), lax.axis_index("c")
    length = lengths_ref[order_ref[yh * (NRESP // 2) + z // 2]]
    return jnp.clip(length - ((z % 2) * 2 + c) * ROWS, 0, ROWS)


def key_code():
    z = lax.axis_index("z")
    return (z // 2) * SLOT + (z % 2) * 2 * ROWS + lax.broadcasted_iota(jnp.int32, (2 * ROWS, 1), 0)


def row_code(info):
    first = (lax.broadcasted_iota(jnp.int32, (16, HD), 1) == 0).astype(BF16)
    return nt(first, info)[:1].astype(jnp.int32)


def seen_of(info):
    keys, rows = key_code(), row_code(info)
    return (rows >= keys) & (rows // SLOT == keys // SLOT)


def first_kernel(lengths_ref, order_ref, rows_ref, kv_ref, resp_ref, q_ref, g_ref, info_ref, stat_ref):
    q_ref[...] = jnp.zeros_like(q_ref)
    g_ref[...] = jnp.zeros_like(g_ref)
    info_ref[...] = jnp.zeros_like(info_ref)
    c = lax.axis_index("c")
    in_block = lax.broadcasted_iota(jnp.int32, (BLOCK, HD), 0)

    def pack(z, at):
        live = live_rows(lengths_ref, order_ref, z)
        place = pl.ds(pl.multiple_of(at * 16, 16), BLOCK)
        q_ref[place] = rows_ref[z, 0]
        g_ref[place] = jnp.where(in_block < live * GROUP, rows_ref[z, 1], jnp.zeros((), BF16))
        code = (z // 2) * SLOT + ((z % 2) * 2 + c) * ROWS + in_block // GROUP
        info_ref[place] = code.astype(F32).astype(BF16)
        return at + (live + 1) // 2

    pairs = lax.fori_loop(0, NZ, pack, 0)
    chunks = (pairs * 16 + CHUNK - 1) // CHUNK
    stat_ref[...] = jnp.zeros_like(stat_ref)

    def chunk(i, _):
        place = pl.ds(pl.multiple_of(i * CHUNK, CHUNK), CHUNK)
        q, g = q_ref[place], g_ref[place]
        seen = seen_of(info_ref[place])
        raw = nt(resp_ref[0], q)
        logits = jnp.where(seen, raw * SCALE2, -1e30)
        top = jnp.max(logits, axis=0, keepdims=True)
        top = jnp.maximum(top, -1e29)
        weights = jnp.exp2(logits - top)
        total = jnp.sum(weights, axis=0, keepdims=True)
        inner = jnp.sum(weights * nt(resp_ref[1], g), axis=0, keepdims=True)
        for s in range(SHARDS):
            for b in range(PROMPT_DEV // KEYS):
                logits = nt(kv_ref[s, b * KEYS : (b + 1) * KEYS], q) * SCALE2
                dprob = nt(kv_ref[s, PROMPT_DEV + b * KEYS : PROMPT_DEV + (b + 1) * KEYS], g)
                now = jnp.maximum(top, jnp.max(logits, axis=0, keepdims=True))
                weights = jnp.exp2(logits - now)
                factor = jnp.exp2(top - now)
                total = total * factor + jnp.sum(weights, axis=0, keepdims=True)
                inner = inner * factor + jnp.sum(weights * dprob, axis=0, keepdims=True)
                top = now
        stat_ref[pl.ds(i, 1)] = top + jnp.log2(total)
        stat_ref[pl.ds(CHUNKS + i, 1)] = inner / total
        return 0

    lax.fori_loop(0, chunks, chunk, 0)


def second_kernel(
    lengths_ref,
    order_ref,
    stats_ref,
    q_ref,
    g_ref,
    info_ref,
    kv_ref,
    resp_ref,
    qg_ref,
    kvg_ref,
    rg_ref,
    mix_ref,
    keyt_ref,
    kacc_ref,
    vacc_ref,
    racc_ref,
    qacc_ref,
):
    logs = stats_ref[:, :CHUNKS]
    top = jnp.max(logs, axis=0)
    weights = jnp.exp2(logs - top[None])
    total = jnp.sum(weights, axis=0)
    mix_ref[:CHUNKS] = top + jnp.log2(total)
    mix_ref[CHUNKS:] = jnp.sum(weights * stats_ref[:, CHUNKS:], axis=0) / total
    for s in range(SHARDS):
        keyt_ref[s] = kv_ref[s, :PROMPT_DEV].T
    kacc_ref[...] = jnp.zeros_like(kacc_ref)
    vacc_ref[...] = jnp.zeros_like(vacc_ref)
    racc_ref[...] = jnp.zeros_like(racc_ref)
    pairs = lax.fori_loop(
        0, NZ, lambda z, at: at + (live_rows(lengths_ref, order_ref, z) + 1) // 2, 0
    )
    chunks = (pairs * 16 + CHUNK - 1) // CHUNK

    def chunk(i, _):
        place = pl.ds(pl.multiple_of(i * CHUNK, CHUNK), CHUNK)
        q, g = q_ref[place], g_ref[place]
        log, delta = mix_ref[pl.ds(i, 1)], mix_ref[pl.ds(CHUNKS + i, 1)]
        seen = seen_of(info_ref[place])
        prob = jnp.where(seen, jnp.exp2(jnp.where(seen, nt(resp_ref[0], q) * SCALE2 - log, 0.0)), 0.0)
        dscore = (prob * (nt(resp_ref[1], g) - delta)).astype(BF16)
        racc_ref[0] += nn(dscore, q)
        racc_ref[1] += nn(prob.astype(BF16), g)
        qgrad = lax.dot_general(
            resp_ref[0], dscore, (((0,), (0,)), ((), ())), preferred_element_type=F32
        )
        for s in range(SHARDS):
            for b in range(PROMPT_DEV // KEYS):
                at = slice(b * KEYS, (b + 1) * KEYS)
                logits = nt(kv_ref[s, at], q) * SCALE2
                dprob = nt(kv_ref[s, PROMPT_DEV + b * KEYS : PROMPT_DEV + (b + 1) * KEYS], g)
                prob = jnp.exp2(logits - log)
                dscore = (prob * (dprob - delta)).astype(BF16)
                kacc_ref[s, at] += nn(dscore, q)
                vacc_ref[s, at] += nn(prob.astype(BF16), g)
                qgrad = qgrad + nn(keyt_ref[s, :, at], dscore)
        qacc_ref[place] = (qgrad * SCALE).T
        return 0

    lax.fori_loop(0, chunks, chunk, 0)
    in_block = lax.broadcasted_iota(jnp.int32, (BLOCK, HD), 0)

    def unpack(z, at):
        live = live_rows(lengths_ref, order_ref, z)
        block = qacc_ref[pl.ds(pl.multiple_of(at * 16, 16), BLOCK)]
        qg_ref[pl.ds(pl.multiple_of(z * BLOCK, BLOCK), BLOCK)] = jnp.where(
            in_block < live * GROUP, block, 0.0
        ).astype(BF16)
        return at + (live + 1) // 2

    lax.fori_loop(0, NZ, unpack, 0)
    kvg_ref[:, :PROMPT_DEV] = (kacc_ref[...] * SCALE).astype(BF16)
    kvg_ref[:, PROMPT_DEV:] = vacc_ref[...].astype(BF16)
    rg_ref[0] = racc_ref[0] * SCALE
    rg_ref[1] = racc_ref[1]


def shards(
    queries, out_grad, resp_keys, resp_values, prompt_keys, prompt_values, resp_lengths, resp_order
):
    vmem = pl.BlockSpec(memory_space=pltpu.VMEM)
    smem = pl.BlockSpec(memory_space=pltpu.SMEM)
    params = pltpu.CompilerParams(vmem_limit_bytes=48 * 1024 * 1024)
    kv = lax.all_gather(jnp.concatenate([prompt_keys, prompt_values], axis=0), ("yh", "c"))
    resp = lax.all_gather(jnp.stack([resp_keys, resp_values]), "c", axis=1, tiled=True)
    both = jnp.stack(
        [queries.reshape(KVH, GROUP, HD), out_grad.reshape(KVH, GROUP, HD)], axis=1
    )
    both = lax.all_to_all(both, "head", 0, 0, tiled=True)
    both = both.transpose(1, 0, 2, 3).reshape(2, BLOCK, HD)
    rows = lax.all_to_all(
        jnp.broadcast_to(both[None], (NZ, 2, BLOCK, HD)), "z", 0, 0, tiled=True
    )
    packed = jax.ShapeDtypeStruct((CLASS + BLOCK, HD), BF16)
    q, g, info, stat = pl.pallas_call(
        first_kernel,
        out_shape=(packed, packed, packed, jax.ShapeDtypeStruct((2 * CHUNKS, CHUNK), F32)),
        in_specs=[smem, smem, vmem, vmem, vmem],
        out_specs=(vmem, vmem, vmem, vmem),
        compiler_params=params,
        name="first_pass",
    )(resp_lengths, resp_order, rows, kv, resp)
    stats = lax.all_to_all(
        jnp.broadcast_to(stat[None], (NZ,) + stat.shape), "z", 0, 0, tiled=True
    )
    accum = pltpu.VMEM((SHARDS, PROMPT_DEV, HD), F32)
    qg, kvg, rg = pl.pallas_call(
        second_kernel,
        out_shape=(
            jax.ShapeDtypeStruct((CLASS, HD), BF16),
            jax.ShapeDtypeStruct((SHARDS, 2 * PROMPT_DEV, HD), BF16),
            jax.ShapeDtypeStruct((2, 2 * ROWS, HD), F32),
        ),
        in_specs=[smem, smem] + [vmem] * 6,
        out_specs=(vmem, vmem, vmem),
        scratch_shapes=[
            pltpu.VMEM((2 * CHUNKS, CHUNK), F32),
            pltpu.VMEM((SHARDS, HD, PROMPT_DEV), BF16),
            accum,
            accum,
            pltpu.VMEM((2, 2 * ROWS, HD), F32),
            pltpu.VMEM((CLASS + BLOCK, HD), F32),
        ],
        compiler_params=params,
        name="second_pass",
    )(resp_lengths, resp_order, stats, q, g, info, kv, resp)
    terms = lax.all_to_all(
        qg.reshape(NZ * KVH, GROUP, HD), ("z", "head"), 0, 0, tiled=True
    )
    query_grad = (
        jnp.sum(terms.reshape(NZ, QH, HD), axis=0, dtype=F32).astype(BF16).reshape(1, QH * HD)
    )
    c = lax.axis_index("c")
    yh = lax.axis_index("yh")
    swap = [(0, 1), (1, 0)]
    kvg = kvg.reshape(2, 2, 2 * PROMPT_DEV, HD)
    mine = lax.dynamic_index_in_dim(kvg, c, 1, keepdims=False)
    other = lax.dynamic_index_in_dim(kvg, 1 - c, 1, keepdims=False)
    mine = mine.astype(F32) + lax.ppermute(other, "c", swap)
    near = lax.dynamic_index_in_dim(mine, yh, 0, keepdims=False)
    far = lax.dynamic_index_in_dim(mine, 1 - yh, 0, keepdims=False).astype(BF16)
    grads = (near + lax.ppermute(far, "yh", swap)).astype(BF16)
    rg = rg.reshape(2, 2, ROWS, HD)
    resp_mine = lax.dynamic_index_in_dim(rg, c, 1, keepdims=False)
    resp_other = lax.dynamic_index_in_dim(rg, 1 - c, 1, keepdims=False)
    resp_grads = (resp_mine + lax.ppermute(resp_other, "c", swap)).astype(BF16)
    return (
        query_grad,
        grads[:PROMPT_DEV],
        grads[PROMPT_DEV:],
        resp_grads[0],
        resp_grads[1],
    )


def solution(mesh):
    fine = Mesh(mesh.devices.reshape(2, NZ, 2, KVH), ("yh", "z", "c", "head"))
    ctx = ("yh", "z", "c")
    row = P(ctx + ("head",), None)
    col = P(ctx, "head")
    return jax.shard_map(
        shards,
        mesh=fine,
        in_specs=(row, row, col, col, col, col, P(), P()),
        out_specs=(row, col, col, col, col),
        check_vma=False,
    )
```

```python
import math

import jax
import jax.numpy as jnp
from jax import lax
from jax.experimental import pallas as pl
from jax.experimental.pallas import tpu as pltpu
from jax.sharding import Mesh
from jax.sharding import PartitionSpec as P

QH = 64
KVH = 8
HD = 128
NRESP = 16
GROUP = QH // KVH
SLOT = 32
NZ = 16
ROWS = 8
BLOCK = ROWS * GROUP
CLASS = NZ * BLOCK
CHUNK = 256
CHUNKS = CLASS // CHUNK
PROMPT_DEV = 768
KEYS = 384
OWN_KEYS = 256
WIDE = 2
SCALE = 1.0 / math.sqrt(HD)
SCALE2 = SCALE * math.log2(math.e)
F32 = jnp.float32
BF16 = jnp.bfloat16


def nt(a, b):
    return lax.dot_general(a, b, (((1,), (1,)), ((), ())), preferred_element_type=F32)


def nn(a, b):
    return jnp.dot(a, b, preferred_element_type=F32)


def live_rows(lengths_ref, order_ref, yh, c, z):
    length = lengths_ref[order_ref[yh * (NRESP // 2) + z // 2]]
    return jnp.clip(length - ((z % 2) * 2 + c) * ROWS, 0, ROWS)


def pack_rows(lengths_ref, order_ref, rows_ref, yh, c, near, start, q_ref, g_ref, info_ref):
    in_block = lax.broadcasted_iota(jnp.int32, (BLOCK, HD), 0)
    at = start * (CHUNK // 16)
    for z in range(NZ):
        live = live_rows(lengths_ref, order_ref, yh, c, z)
        place = pl.ds(pl.multiple_of(at * 16, 16), BLOCK)
        both = rows_ref[z * ROWS : (z + 1) * ROWS].astype(F32)
        q_ref[place] = both[:, :GROUP].reshape(BLOCK, HD).astype(BF16)
        g = both[:, GROUP:].reshape(BLOCK, HD)
        g_ref[place] = jnp.where(in_block < live * GROUP, g, 0.0).astype(BF16)
        if near:
            code = (z // 2) * SLOT + ((z % 2) * 2 + c) * ROWS + in_block // GROUP
            info_ref[place] = code.astype(F32).astype(BF16)
        at = at + (live + 1) // 2
    rest = pl.ds(pl.multiple_of(at * 16, 16), 2 * CHUNK)
    q_ref[rest] = jnp.zeros((2 * CHUNK, HD), BF16)
    g_ref[rest] = jnp.zeros((2 * CHUNK, HD), BF16)
    if near:
        info_ref[rest] = jnp.full((2 * CHUNK, HD), -SLOT, BF16)
    return (at * 16 + CHUNK - 1) // CHUNK


def unpack_rows(lengths_ref, order_ref, yh, c, acc_ref, out_ref):
    in_block = lax.broadcasted_iota(jnp.int32, (BLOCK, HD), 0)
    at = 0
    for z in range(NZ):
        live = live_rows(lengths_ref, order_ref, yh, c, z)
        block = acc_ref[pl.ds(pl.multiple_of(at * 16, 16), BLOCK)]
        out_ref[z * BLOCK : (z + 1) * BLOCK] = jnp.where(
            in_block < live * GROUP, block, 0.0
        ).astype(BF16)
        at = at + (live + 1) // 2


def key_code(z, c):
    at = lax.broadcasted_iota(jnp.int32, (ROWS, 1), 0)
    return (z // 2) * SLOT + ((z % 2) * 2 + c) * ROWS + at


def row_code(info):
    first = (lax.broadcasted_iota(jnp.int32, (16, HD), 1) == 0).astype(BF16)
    return nt(first, info)[:1].astype(jnp.int32)


def seen_of(rows, keys):
    return (rows >= keys) & (rows < (keys // SLOT + 1) * SLOT)


def stack8(a, b):
    return jnp.concatenate([a.astype(F32), b.astype(F32)], axis=0).astype(BF16)


def send_kernel(q_hbm, g_hbm, rows_ref, q_ref, g_ref, hold_ref, sems):
    copies = [
        pltpu.make_async_copy(q_hbm, q_ref, sems.at[0]),
        pltpu.make_async_copy(g_hbm, g_ref, sems.at[1]),
    ]
    for copy in copies:
        copy.start()
    for copy in copies:
        copy.wait()
    for h in range(QH):
        at = slice(h * HD, (h + 1) * HD)
        hold_ref[h // GROUP, h % GROUP : h % GROUP + 1] = q_ref[:, at].astype(F32)
        hold_ref[h // GROUP, GROUP + h % GROUP : GROUP + h % GROUP + 1] = g_ref[:, at].astype(F32)
    for z in range(NZ):
        rows_ref[z * KVH : (z + 1) * KVH] = hold_ref[...].astype(BF16)


def keys_kernel(k_hbm, v_hbm, rk_hbm, rv_hbm, kv_ref, rk_ref, rv_ref, sems):
    copies = [
        pltpu.make_async_copy(k_hbm, kv_ref.at[:PROMPT_DEV], sems.at[0]),
        pltpu.make_async_copy(v_hbm, kv_ref.at[PROMPT_DEV : 2 * PROMPT_DEV], sems.at[1]),
        pltpu.make_async_copy(rk_hbm, rk_ref, sems.at[2]),
        pltpu.make_async_copy(rv_hbm, rv_ref, sems.at[3]),
    ]
    for copy in copies:
        copy.start()
    for copy in copies:
        copy.wait()
    kv_ref[2 * PROMPT_DEV :] = stack8(rk_ref[...], rv_ref[...])


def resp_of(kv_ref):
    a, b = (kv_ref[c, 2 * PROMPT_DEV :].astype(F32) for c in range(2))
    keys = jnp.concatenate([a[:ROWS], b[:ROWS]], axis=0).astype(BF16)
    values = jnp.concatenate([a[ROWS:], b[ROWS:]], axis=0).astype(BF16)
    return keys, values


def lanes_of(ref, first, count):
    return jnp.concatenate([ref[i : i + 1] for i in range(first, first + count)], axis=1)


def key_parts(near_ref, far_ref):
    return [
        (ref, c, b) for ref in (near_ref, far_ref) for c in range(2) for b in range(0, PROMPT_DEV, KEYS)
    ]


def first_kernel(
    lengths_ref,
    order_ref,
    rows_ref,
    near_kv_ref,
    far_kv_ref,
    out_ref,
    stat_ref,
    q_ref,
    g_ref,
    info_ref,
    near_ref,
):
    yh, c, z = lax.axis_index("yh"), lax.axis_index("c"), lax.axis_index("z")
    chunks = pack_rows(
        lengths_ref, order_ref, rows_ref, yh, c, True, 0, q_ref, g_ref, info_ref
    )
    stat_ref[...] = jnp.zeros_like(stat_ref)
    resp_k, resp_v = resp_of(near_kv_ref)
    keys = jnp.concatenate([key_code(z, 0), key_code(z, 1)], axis=0)
    seen = seen_of(row_code(info_ref[:CLASS]), keys)
    logits = jnp.where(seen, nt(resp_k, q_ref[:CLASS]) * SCALE2, -1e30)
    top = jnp.maximum(jnp.max(logits, axis=0, keepdims=True), -1e29)
    weights = jnp.exp2(logits - top)
    total = jnp.sum(weights, axis=0, keepdims=True)
    inner = jnp.sum(weights * nt(resp_v, g_ref[:CLASS]), axis=0, keepdims=True)
    for i in range(CHUNKS):
        lanes = slice(i * CHUNK, (i + 1) * CHUNK)
        near_ref[0, i : i + 1] = top[:, lanes]
        near_ref[1, i : i + 1] = total[:, lanes]
        near_ref[2, i : i + 1] = inner[:, lanes]

    def chunk(i, _):
        place = pl.ds(pl.multiple_of(i * CHUNK, CHUNK), CHUNK)
        q, g = q_ref[place], g_ref[place]
        top, total, inner = (near_ref[n, pl.ds(i, 1)] for n in range(3))
        for ref, k, b in key_parts(near_kv_ref, far_kv_ref):
            logits = nt(ref[k, b : b + KEYS], q) * SCALE2
            dprob = nt(ref[k, PROMPT_DEV + b : PROMPT_DEV + b + KEYS], g)
            now = jnp.maximum(top, jnp.max(logits, axis=0, keepdims=True))
            weights = jnp.exp2(logits - now)
            factor = jnp.exp2(top - now)
            total = total * factor + jnp.sum(weights, axis=0, keepdims=True)
            inner = inner * factor + jnp.sum(weights * dprob, axis=0, keepdims=True)
            top = now
        stat_ref[pl.ds(i, 1)] = top + jnp.log2(total)
        stat_ref[pl.ds(CHUNKS + i, 1)] = inner / total
        return 0

    lax.fori_loop(0, chunks, chunk, 0)
    for n in range(NZ):
        out_ref[n] = stat_ref[...]


def query_kernel(
    lengths_ref,
    order_ref,
    stats_ref,
    rows_ref,
    near_kv_ref,
    far_kv_ref,
    mix_ref,
    qg_ref,
    q_ref,
    g_ref,
    info_ref,
    near_ref,
    keyt_ref,
    qacc_ref,
):
    yh, c, z = lax.axis_index("yh"), lax.axis_index("c"), lax.axis_index("z")
    logs = stats_ref[:, :CHUNKS]
    top = jnp.max(logs, axis=0)
    weights = jnp.exp2(logs - top[None])
    total = jnp.sum(weights, axis=0)
    mix_ref[:CHUNKS] = top + jnp.log2(total)
    mix_ref[CHUNKS:] = jnp.sum(weights * stats_ref[:, CHUNKS:], axis=0) / total
    for n, (ref, k, b) in enumerate(key_parts(near_kv_ref, far_kv_ref)):
        keyt_ref[n] = ref[k, b : b + KEYS].T
    chunks = pack_rows(
        lengths_ref, order_ref, rows_ref, yh, c, True, 0, q_ref, g_ref, info_ref
    )
    resp_k, resp_v = resp_of(near_kv_ref)
    keys = jnp.concatenate([key_code(z, 0), key_code(z, 1)], axis=0)
    seen = seen_of(row_code(info_ref[:CLASS]), keys)
    log, delta = lanes_of(mix_ref, 0, CHUNKS), lanes_of(mix_ref, CHUNKS, CHUNKS)
    prob = jnp.exp2(jnp.where(seen, nt(resp_k, q_ref[:CLASS]) * SCALE2 - log, -1e30))
    near_ref[...] = (prob * (nt(resp_v, g_ref[:CLASS]) - delta)).astype(BF16).T

    def chunk(i, _):
        place = pl.ds(pl.multiple_of(i * CHUNK, CHUNK), CHUNK)
        q, g = q_ref[place], g_ref[place]
        log, delta = mix_ref[pl.ds(i, 1)], mix_ref[pl.ds(CHUNKS + i, 1)]
        qgrad = jnp.zeros((HD, CHUNK), F32)
        for n, (ref, k, b) in enumerate(key_parts(near_kv_ref, far_kv_ref)):
            prob = jnp.exp2(nt(ref[k, b : b + KEYS], q) * SCALE2 - log)
            dprob = nt(ref[k, PROMPT_DEV + b : PROMPT_DEV + b + KEYS], g)
            qgrad = qgrad + nn(keyt_ref[n], (prob * (dprob - delta)).astype(BF16))
        qacc_ref[place] = (qgrad.T + nn(near_ref[place], resp_k)) * SCALE
        return 0

    lax.fori_loop(0, chunks, chunk, 0)
    unpack_rows(lengths_ref, order_ref, yh, c, qacc_ref, qg_ref)


def key_kernel(
    lengths_ref,
    order_ref,
    mix_ref,
    rows_ref,
    rows_c_ref,
    rows_y_ref,
    rows_yc_ref,
    own_ref,
    kg_ref,
    vg_ref,
    rkg_ref,
    rvg_ref,
    q_ref,
    g_ref,
    info_ref,
    log_ref,
    delta_ref,
    kacc_ref,
    vacc_ref,
):
    yh, c, z = lax.axis_index("yh"), lax.axis_index("c"), lax.axis_index("z")
    kacc_ref[...] = jnp.zeros_like(kacc_ref)
    vacc_ref[...] = jnp.zeros_like(vacc_ref)
    log_ref[...] = jnp.zeros_like(log_ref)
    delta_ref[...] = jnp.zeros_like(delta_ref)
    chunks = 0
    for far, cross, ref in (
        (0, 0, rows_ref),
        (0, 1, rows_c_ref),
        (1, 0, rows_y_ref),
        (1, 1, rows_yc_ref),
    ):
        its_yh, its_c = (1 - yh if far else yh), (1 - c if cross else c)
        its = its_yh * 2 + its_c
        for i in range(CHUNKS):
            log_ref[pl.ds(chunks + i, 1)] = mix_ref[its, i : i + 1]
            delta_ref[pl.ds(chunks + i, 1)] = mix_ref[its, CHUNKS + i : CHUNKS + i + 1]
        chunks = pack_rows(
            lengths_ref, order_ref, ref, its_yh, its_c, not far, chunks, q_ref, g_ref, info_ref
        )
        if not far:
            info_ref[pl.ds(pl.multiple_of(chunks * CHUNK, CHUNK), CLASS)] = jnp.full(
                (CLASS, HD), -SLOT, BF16
            )
    resp = own_ref[2 * PROMPT_DEV :]
    none = jnp.zeros((ROWS, HD), F32)
    resp_k = jnp.concatenate([resp[:ROWS].astype(F32), none], axis=0).astype(BF16)
    resp_v = jnp.concatenate([resp[ROWS:].astype(F32), none], axis=0).astype(BF16)
    keys = jnp.concatenate([key_code(z, c), jnp.full((ROWS, 1), 1 << 20, jnp.int32)], axis=0)
    seen = seen_of(row_code(info_ref[: 2 * CLASS]), keys)
    log, delta = lanes_of(log_ref, 0, 2 * CHUNKS), lanes_of(delta_ref, 0, 2 * CHUNKS)
    q, g = q_ref[: 2 * CLASS], g_ref[: 2 * CLASS]
    prob = jnp.exp2(jnp.where(seen, nt(resp_k, q) * SCALE2 - log, -1e30))
    dscore = (prob * (nt(resp_v, g) - delta)).astype(BF16)
    rkg_ref[...] = (nn(dscore, q)[:ROWS] * SCALE).astype(BF16)
    rvg_ref[...] = nn(prob.astype(BF16), g)[:ROWS].astype(BF16)

    def step(n, _):
        place = pl.ds(pl.multiple_of(n * WIDE * CHUNK, CHUNK), WIDE * CHUNK)
        q, g = q_ref[place], g_ref[place]
        log = jnp.concatenate([log_ref[pl.ds(WIDE * n + i, 1)] for i in range(WIDE)], axis=1)
        delta = jnp.concatenate([delta_ref[pl.ds(WIDE * n + i, 1)] for i in range(WIDE)], axis=1)
        for b in range(0, PROMPT_DEV, OWN_KEYS):
            prob = jnp.exp2(nt(own_ref[b : b + OWN_KEYS], q) * SCALE2 - log)
            dprob = nt(own_ref[PROMPT_DEV + b : PROMPT_DEV + b + OWN_KEYS], g)
            dscore = (prob * (dprob - delta)).astype(BF16)
            kacc_ref[b : b + OWN_KEYS] += nn(dscore, q)
            vacc_ref[b : b + OWN_KEYS] += nn(prob.astype(BF16), g)
        return 0

    lax.fori_loop(0, (chunks + WIDE - 1) // WIDE, step, 0)
    kg_ref[...] = (kacc_ref[...] * SCALE).astype(BF16)
    vg_ref[...] = vacc_ref[...].astype(BF16)


def finish_kernel(terms_ref, out_ref):
    total = jnp.sum(terms_ref[...].astype(F32), axis=0)
    for h in range(QH):
        out_ref[:, h * HD : (h + 1) * HD] = total[h : h + 1].astype(BF16)


def shards(
    queries, out_grad, resp_keys, resp_values, prompt_keys, prompt_values, resp_lengths, resp_order
):
    vmem = pl.BlockSpec(memory_space=pltpu.VMEM)
    smem = pl.BlockSpec(memory_space=pltpu.SMEM)
    hbm = pl.BlockSpec(memory_space=pltpu.HBM)
    params = pltpu.CompilerParams(vmem_limit_bytes=32 * 1024 * 1024)
    swap = [(0, 1), (1, 0)]
    shape = jax.ShapeDtypeStruct

    def call(kernel, name, out_shape, ints, arrays, scratch=(), space=vmem):
        return pl.pallas_call(
            kernel,
            out_shape=out_shape,
            in_specs=[smem] * len(ints) + [space] * len(arrays),
            out_specs=jax.tree.map(lambda _: vmem, out_shape),
            scratch_shapes=list(scratch),
            compiler_params=params,
            name=name,
        )(*ints, *arrays)

    whole = pltpu.VMEM((1, QH * HD), BF16)
    rows = call(
        send_kernel,
        "send",
        shape((NZ * KVH, 2 * GROUP, HD), BF16),
        (),
        (queries, out_grad),
        [whole, whole, pltpu.VMEM((KVH, 2 * GROUP, HD), F32), pltpu.SemaphoreType.DMA((2,))],
        hbm,
    )
    few = pltpu.VMEM((ROWS, HD), BF16)
    kv = call(
        keys_kernel,
        "keys",
        shape((2 * PROMPT_DEV + 2 * ROWS, HD), BF16),
        (),
        (prompt_keys, prompt_values, resp_keys, resp_values),
        [few, few, pltpu.SemaphoreType.DMA((4,))],
        hbm,
    )
    near_kv = lax.all_gather(kv, "c")
    far_kv = lax.all_gather(lax.ppermute(kv, "yh", swap), "c")
    rows = lax.all_to_all(rows, ("z", "head"), 0, 0, tiled=True)
    packed = pltpu.VMEM((CLASS + BLOCK + 2 * CHUNK, HD), BF16)
    ints = (resp_lengths, resp_order)
    stats = call(
        first_kernel,
        "first_pass",
        shape((NZ, 2 * CHUNKS, CHUNK), F32),
        ints,
        (rows, near_kv, far_kv),
        [
            pltpu.VMEM((2 * CHUNKS, CHUNK), F32),
            packed,
            packed,
            packed,
            pltpu.VMEM((3, 2 * CHUNKS, CHUNK), F32),
        ],
    )
    stats, rows = lax.optimization_barrier((stats, rows))
    rows_c = lax.ppermute(rows, "c", swap)
    rows_y = lax.ppermute(rows, "yh", swap)
    rows_yc = lax.ppermute(rows_y, "c", swap)
    stats = lax.all_to_all(stats, "z", 0, 0, tiled=True)
    stats, rows_c = lax.optimization_barrier((stats, rows_c))
    mix, qg = call(
        query_kernel,
        "query_pass",
        (shape((2 * CHUNKS, CHUNK), F32), shape((CLASS, HD), BF16)),
        ints,
        (stats, rows, near_kv, far_kv),
        [
            packed,
            packed,
            packed,
            pltpu.VMEM((CLASS, 2 * ROWS), BF16),
            pltpu.VMEM((4 * PROMPT_DEV // KEYS, HD, KEYS), BF16),
            pltpu.VMEM((CLASS + BLOCK, HD), F32),
        ],
    )
    terms = lax.all_to_all(
        qg.reshape(NZ * KVH, GROUP, HD), ("z", "head"), 0, 0, tiled=True
    )
    mixes = lax.all_gather(mix, ("yh", "c"))
    acc = pltpu.VMEM((PROMPT_DEV, HD), F32)
    everyone = pltpu.VMEM((4 * CLASS + BLOCK + 2 * CHUNK, HD), BF16)
    per_chunk = pltpu.VMEM((6 * CHUNKS, CHUNK), F32)
    key_grad, value_grad, resp_key_grad, resp_value_grad = call(
        key_kernel,
        "key_pass",
        (
            shape((PROMPT_DEV, HD), BF16),
            shape((PROMPT_DEV, HD), BF16),
            shape((ROWS, HD), BF16),
            shape((ROWS, HD), BF16),
        ),
        ints,
        (mixes, rows, rows_c, rows_y, rows_yc, kv),
        [everyone, everyone, everyone, per_chunk, per_chunk, acc, acc],
    )
    query_grad = call(
        finish_kernel, "finish", shape((1, QH * HD), BF16), (), (terms.reshape(NZ, QH, HD),)
    )
    return query_grad, key_grad, value_grad, resp_key_grad, resp_value_grad


def solution(mesh):
    fine = Mesh(mesh.devices.reshape(2, NZ, 2, KVH), ("yh", "z", "c", "head"))
    ctx = ("yh", "z", "c")
    row = P(ctx + ("head",), None)
    col = P(ctx, "head")
    return jax.shard_map(
        shards,
        mesh=fine,
        in_specs=(row, row, col, col, col, col, P(), P()),
        out_specs=(row, col, col, col, col),
        check_vma=False,
    )
```

```python
import functools
import math

import jax
import jax.numpy as jnp
from jax import lax
from jax.experimental import pallas as pl
from jax.experimental.pallas import tpu as pltpu
from jax.sharding import Mesh
from jax.sharding import PartitionSpec as P

QH = 64
KVH = 8
HD = 128
NRESP = 16
GROUP = QH // KVH
SLOT = 32
NZ = 16
ROWS = 8
BLOCK = ROWS * GROUP
CLASS = NZ * BLOCK
CHUNK = 256
CHUNKS = CLASS // CHUNK
PROMPT_DEV = 768
KEYS1 = 256
KEYS2 = 768
WIDE = 2
SCALE = 1.0 / math.sqrt(HD)
SCALE2 = SCALE * math.log2(math.e)
ROW_FLOPS = 5 * 10**9
KEY_FLOPS = 40 * 10**9
F32 = jnp.float32
BF16 = jnp.bfloat16


def nt(a, b):
    return lax.dot_general(a, b, (((1,), (1,)), ((), ())), preferred_element_type=F32)


def nn(a, b):
    return jnp.dot(a, b, preferred_element_type=F32)


def live_rows(lengths_ref, order_ref, yh, c, z):
    length = lengths_ref[order_ref[yh * (NRESP // 2) + z // 2]]
    return jnp.clip(length - ((z % 2) * 2 + c) * ROWS, 0, ROWS)


def pack_rows(lengths_ref, order_ref, rows_ref, yh, c, near, start, q_ref, g_ref, info_ref):
    in_block = lax.broadcasted_iota(jnp.int32, (BLOCK, HD), 0)
    at = start * (CHUNK // 16)
    for z in range(NZ):
        live = live_rows(lengths_ref, order_ref, yh, c, z)
        place = pl.ds(pl.multiple_of(at * 16, 16), BLOCK)
        both = rows_ref[z * ROWS : (z + 1) * ROWS].astype(F32)
        q_ref[place] = both[:, :GROUP].reshape(BLOCK, HD).astype(BF16)
        g = both[:, GROUP:].reshape(BLOCK, HD)
        g_ref[place] = jnp.where(in_block < live * GROUP, g, 0.0).astype(BF16)
        if near:
            code = (z // 2) * SLOT + ((z % 2) * 2 + c) * ROWS + in_block // GROUP
            info_ref[place] = code.astype(F32).astype(BF16)
        at = at + (live + 1) // 2
    rest = pl.ds(pl.multiple_of(at * 16, 16), 2 * CHUNK)
    q_ref[rest] = jnp.zeros((2 * CHUNK, HD), BF16)
    g_ref[rest] = jnp.zeros((2 * CHUNK, HD), BF16)
    if near:
        info_ref[rest] = jnp.full((2 * CHUNK, HD), -SLOT, BF16)
    return (at * 16 + CHUNK - 1) // CHUNK


def unpack_rows(lengths_ref, order_ref, yh, c, acc_ref, out_ref):
    in_block = lax.broadcasted_iota(jnp.int32, (BLOCK, HD), 0)
    at = 0
    for z in range(NZ):
        live = live_rows(lengths_ref, order_ref, yh, c, z)
        block = acc_ref[pl.ds(pl.multiple_of(at * 16, 16), BLOCK)]
        out_ref[z * BLOCK : (z + 1) * BLOCK] = jnp.where(
            in_block < live * GROUP, block, 0.0
        ).astype(BF16)
        at = at + (live + 1) // 2


def key_code(z, c):
    at = lax.broadcasted_iota(jnp.int32, (ROWS, 1), 0)
    return (z // 2) * SLOT + ((z % 2) * 2 + c) * ROWS + at


def row_code(info):
    first = (lax.broadcasted_iota(jnp.int32, (16, HD), 1) == 0).astype(BF16)
    return nt(first, info)[:1].astype(jnp.int32)


def seen_of(rows, keys):
    return (rows >= keys) & (rows < (keys // SLOT + 1) * SLOT)


def stack8(a, b):
    return jnp.concatenate([a.astype(F32), b.astype(F32)], axis=0).astype(BF16)


def send_kernel(q_hbm, g_hbm, rows_ref, q_ref, g_ref, hold_ref, sems):
    copies = [
        pltpu.make_async_copy(q_hbm, q_ref, sems.at[0]),
        pltpu.make_async_copy(g_hbm, g_ref, sems.at[1]),
    ]
    for copy in copies:
        copy.start()
    for copy in copies:
        copy.wait()
    for h in range(QH):
        at = slice(h * HD, (h + 1) * HD)
        hold_ref[h // GROUP, h % GROUP : h % GROUP + 1] = q_ref[:, at].astype(F32)
        hold_ref[h // GROUP, GROUP + h % GROUP : GROUP + h % GROUP + 1] = g_ref[:, at].astype(F32)
    for z in range(NZ):
        rows_ref[z * KVH : (z + 1) * KVH] = hold_ref[...].astype(BF16)


def keys_kernel(k_hbm, v_hbm, rk_hbm, rv_hbm, kv_ref, rk_ref, rv_ref, sems):
    copies = [
        pltpu.make_async_copy(k_hbm, kv_ref.at[:PROMPT_DEV], sems.at[0]),
        pltpu.make_async_copy(v_hbm, kv_ref.at[PROMPT_DEV : 2 * PROMPT_DEV], sems.at[1]),
        pltpu.make_async_copy(rk_hbm, rk_ref, sems.at[2]),
        pltpu.make_async_copy(rv_hbm, rv_ref, sems.at[3]),
    ]
    for copy in copies:
        copy.start()
    for copy in copies:
        copy.wait()
    kv_ref[2 * PROMPT_DEV :] = stack8(rk_ref[...], rv_ref[...])


def resp_of(kv_ref):
    a, b = (kv_ref[c, 2 * PROMPT_DEV :].astype(F32) for c in range(2))
    keys = jnp.concatenate([a[:ROWS], b[:ROWS]], axis=0).astype(BF16)
    values = jnp.concatenate([a[ROWS:], b[ROWS:]], axis=0).astype(BF16)
    return keys, values


def lanes_of(ref, first, count):
    return jnp.concatenate([ref[i : i + 1] for i in range(first, first + count)], axis=1)


def key_parts(near_ref, far_ref, step):
    return [
        (ref, c, b) for ref in (near_ref, far_ref) for c in range(2) for b in range(0, PROMPT_DEV, step)
    ]


def first_kernel(
    lengths_ref,
    order_ref,
    rows_ref,
    near_kv_ref,
    far_kv_ref,
    out_ref,
    stat_ref,
    q_ref,
    g_ref,
    info_ref,
    near_ref,
):
    yh, c, z = lax.axis_index("yh"), lax.axis_index("c"), lax.axis_index("z")
    chunks = pack_rows(
        lengths_ref, order_ref, rows_ref, yh, c, True, 0, q_ref, g_ref, info_ref
    )
    stat_ref[...] = jnp.zeros_like(stat_ref)
    resp_k, resp_v = resp_of(near_kv_ref)
    keys = jnp.concatenate([key_code(z, 0), key_code(z, 1)], axis=0)
    seen = seen_of(row_code(info_ref[:CLASS]), keys)
    logits = jnp.where(seen, nt(resp_k, q_ref[:CLASS]) * SCALE2, -1e30)
    top = jnp.maximum(jnp.max(logits, axis=0, keepdims=True), -1e29)
    weights = jnp.exp2(logits - top)
    total = jnp.sum(weights, axis=0, keepdims=True)
    inner = jnp.sum(weights * nt(resp_v, g_ref[:CLASS]), axis=0, keepdims=True)
    for i in range(CHUNKS):
        lanes = slice(i * CHUNK, (i + 1) * CHUNK)
        near_ref[0, i : i + 1] = top[:, lanes]
        near_ref[1, i : i + 1] = total[:, lanes]
        near_ref[2, i : i + 1] = inner[:, lanes]

    def chunk(i, _):
        place = pl.ds(pl.multiple_of(i * CHUNK, CHUNK), CHUNK)
        q, g = q_ref[place], g_ref[place]
        top, total, inner = (near_ref[n, pl.ds(i, 1)] for n in range(3))
        for ref, k, b in key_parts(near_kv_ref, far_kv_ref, KEYS1):
            logits = nt(ref[k, b : b + KEYS1], q) * SCALE2
            dprob = nt(ref[k, PROMPT_DEV + b : PROMPT_DEV + b + KEYS1], g)
            now = jnp.maximum(top, jnp.max(logits, axis=0, keepdims=True))
            weights = jnp.exp2(logits - now)
            factor = jnp.exp2(top - now)
            total = total * factor + jnp.sum(weights, axis=0, keepdims=True)
            inner = inner * factor + jnp.sum(weights * dprob, axis=0, keepdims=True)
            top = now
        stat_ref[pl.ds(i, 1)] = top + jnp.log2(total)
        stat_ref[pl.ds(CHUNKS + i, 1)] = inner / total
        return 0

    lax.fori_loop(0, chunks, chunk, 0)
    for n in range(NZ):
        out_ref[n] = stat_ref[...]


def query_kernel(
    lengths_ref,
    order_ref,
    stats_ref,
    rows_ref,
    near_kv_ref,
    far_kv_ref,
    mix_ref,
    qg_ref,
    q_ref,
    g_ref,
    info_ref,
    near_ref,
    keyt_ref,
    qacc_ref,
):
    yh, c, z = lax.axis_index("yh"), lax.axis_index("c"), lax.axis_index("z")
    logs = stats_ref[:, :CHUNKS]
    top = jnp.max(logs, axis=0)
    weights = jnp.exp2(logs - top[None])
    total = jnp.sum(weights, axis=0)
    mix_ref[:CHUNKS] = top + jnp.log2(total)
    mix_ref[CHUNKS:] = jnp.sum(weights * stats_ref[:, CHUNKS:], axis=0) / total
    for n, (ref, k, b) in enumerate(key_parts(near_kv_ref, far_kv_ref, KEYS2)):
        keyt_ref[n] = ref[k, b : b + KEYS2].T
    chunks = pack_rows(
        lengths_ref, order_ref, rows_ref, yh, c, True, 0, q_ref, g_ref, info_ref
    )
    resp_k, resp_v = resp_of(near_kv_ref)
    keys = jnp.concatenate([key_code(z, 0), key_code(z, 1)], axis=0)
    seen = seen_of(row_code(info_ref[:CLASS]), keys)
    log, delta = lanes_of(mix_ref, 0, CHUNKS), lanes_of(mix_ref, CHUNKS, CHUNKS)
    prob = jnp.exp2(jnp.where(seen, nt(resp_k, q_ref[:CLASS]) * SCALE2 - log, -1e30))
    near_ref[...] = (prob * (nt(resp_v, g_ref[:CLASS]) - delta)).astype(BF16).T

    def chunk(i, _):
        place = pl.ds(pl.multiple_of(i * CHUNK, CHUNK), CHUNK)
        q, g = q_ref[place], g_ref[place]
        log, delta = mix_ref[pl.ds(i, 1)], mix_ref[pl.ds(CHUNKS + i, 1)]
        qgrad = jnp.zeros((HD, CHUNK), F32)
        for n, (ref, k, b) in enumerate(key_parts(near_kv_ref, far_kv_ref, KEYS2)):
            prob = jnp.exp2(nt(ref[k, b : b + KEYS2], q) * SCALE2 - log)
            dprob = nt(ref[k, PROMPT_DEV + b : PROMPT_DEV + b + KEYS2], g)
            qgrad = qgrad + nn(keyt_ref[n], (prob * (dprob - delta)).astype(BF16))
        qacc_ref[place] = (qgrad.T + nn(near_ref[place], resp_k)) * SCALE
        return 0

    lax.fori_loop(0, chunks, chunk, 0)
    unpack_rows(lengths_ref, order_ref, yh, c, qacc_ref, qg_ref)


def key_kernel(
    cross,
    lengths_ref,
    order_ref,
    mix_ref,
    rows_ref,
    rows_y_ref,
    kv_ref,
    out_ref,
    q_ref,
    g_ref,
    info_ref,
    log_ref,
    delta_ref,
    kacc_ref,
    vacc_ref,
):
    yh, c, z = lax.axis_index("yh"), lax.axis_index("c"), lax.axis_index("z")
    its_c = 1 - c if cross else c
    kacc_ref[...] = jnp.zeros_like(kacc_ref)
    vacc_ref[...] = jnp.zeros_like(vacc_ref)
    log_ref[...] = jnp.zeros_like(log_ref)
    delta_ref[...] = jnp.zeros_like(delta_ref)
    chunks = 0
    for far, ref in ((0, rows_ref), (1, rows_y_ref)):
        its_yh = 1 - yh if far else yh
        for i in range(CHUNKS):
            log_ref[pl.ds(chunks + i, 1)] = mix_ref[its_yh, i : i + 1]
            delta_ref[pl.ds(chunks + i, 1)] = mix_ref[its_yh, CHUNKS + i : CHUNKS + i + 1]
        chunks = pack_rows(
            lengths_ref, order_ref, ref, its_yh, c, not far, chunks, q_ref, g_ref, info_ref
        )
        if not far:
            info_ref[pl.ds(pl.multiple_of(chunks * CHUNK, CHUNK), CLASS)] = jnp.full(
                (CLASS, HD), -SLOT, BF16
            )
    resp = kv_ref[its_c, 2 * PROMPT_DEV :]
    none = jnp.zeros((ROWS, HD), F32)
    resp_k = jnp.concatenate([resp[:ROWS].astype(F32), none], axis=0).astype(BF16)
    resp_v = jnp.concatenate([resp[ROWS:].astype(F32), none], axis=0).astype(BF16)
    keys = jnp.concatenate([key_code(z, its_c), jnp.full((ROWS, 1), 1 << 20, jnp.int32)], axis=0)
    seen = seen_of(row_code(info_ref[:CLASS]), keys)
    log, delta = lanes_of(log_ref, 0, CHUNKS), lanes_of(delta_ref, 0, CHUNKS)
    q, g = q_ref[:CLASS], g_ref[:CLASS]
    prob = jnp.exp2(jnp.where(seen, nt(resp_k, q) * SCALE2 - log, -1e30))
    dscore = (prob * (nt(resp_v, g) - delta)).astype(BF16)
    resp_kg = nn(dscore, q)[:ROWS] * SCALE
    resp_vg = nn(prob.astype(BF16), g)[:ROWS]
    out_ref[2 * PROMPT_DEV :] = jnp.concatenate([resp_kg, resp_vg], axis=0).astype(out_ref.dtype)

    def step(n, _):
        place = pl.ds(pl.multiple_of(n * WIDE * CHUNK, CHUNK), WIDE * CHUNK)
        q, g = q_ref[place], g_ref[place]
        log = jnp.concatenate([log_ref[pl.ds(WIDE * n + i, 1)] for i in range(WIDE)], axis=1)
        delta = jnp.concatenate([delta_ref[pl.ds(WIDE * n + i, 1)] for i in range(WIDE)], axis=1)
        prob = jnp.exp2(nt(kv_ref[its_c, :PROMPT_DEV], q) * SCALE2 - log)
        dprob = nt(kv_ref[its_c, PROMPT_DEV : 2 * PROMPT_DEV], g)
        dscore = (prob * (dprob - delta)).astype(BF16)
        kacc_ref[...] += nn(dscore, q)
        vacc_ref[...] += nn(prob.astype(BF16), g)
        return 0

    lax.fori_loop(0, (chunks + WIDE - 1) // WIDE, step, 0)
    out_ref[:PROMPT_DEV] = (kacc_ref[...] * SCALE).astype(out_ref.dtype)
    out_ref[PROMPT_DEV : 2 * PROMPT_DEV] = vacc_ref[...].astype(out_ref.dtype)


def add_kernel(mine_ref, other_ref, kg_ref, vg_ref, rkg_ref, rvg_ref):
    resp = 2 * PROMPT_DEV
    kg_ref[...] = (mine_ref[:PROMPT_DEV] + other_ref[:PROMPT_DEV].astype(F32)).astype(BF16)
    vg_ref[...] = (mine_ref[PROMPT_DEV:resp] + other_ref[PROMPT_DEV:resp].astype(F32)).astype(BF16)
    rest = mine_ref[resp:] + other_ref[resp:].astype(F32)
    rkg_ref[...] = rest[:ROWS].astype(BF16)
    rvg_ref[...] = rest[ROWS:].astype(BF16)


def finish_kernel(terms_ref, out_ref):
    total = jnp.sum(terms_ref[...].astype(F32), axis=0)
    for h in range(QH):
        out_ref[:, h * HD : (h + 1) * HD] = total[h : h + 1].astype(BF16)


def shards(
    queries, out_grad, resp_keys, resp_values, prompt_keys, prompt_values, resp_lengths, resp_order
):
    vmem = pl.BlockSpec(memory_space=pltpu.VMEM)
    smem = pl.BlockSpec(memory_space=pltpu.SMEM)
    hbm = pl.BlockSpec(memory_space=pltpu.HBM)
    params = pltpu.CompilerParams(vmem_limit_bytes=32 * 1024 * 1024)
    swap = [(0, 1), (1, 0)]
    shape = jax.ShapeDtypeStruct

    def call(kernel, name, out_shape, ints, arrays, scratch=(), space=vmem, flops=0):
        cost = pl.CostEstimate(flops=flops, bytes_accessed=0, transcendentals=0) if flops else None
        return pl.pallas_call(
            kernel,
            out_shape=out_shape,
            in_specs=[smem] * len(ints) + [space] * len(arrays),
            out_specs=jax.tree.map(lambda _: vmem, out_shape),
            scratch_shapes=list(scratch),
            compiler_params=params,
            cost_estimate=cost,
            name=name,
        )(*ints, *arrays)

    whole = pltpu.VMEM((1, QH * HD), BF16)
    rows = call(
        send_kernel,
        "send",
        shape((NZ * KVH, 2 * GROUP, HD), BF16),
        (),
        (queries, out_grad),
        [whole, whole, pltpu.VMEM((KVH, 2 * GROUP, HD), F32), pltpu.SemaphoreType.DMA((2,))],
        hbm,
    )
    few = pltpu.VMEM((ROWS, HD), BF16)
    kv = call(
        keys_kernel,
        "keys",
        shape((2 * PROMPT_DEV + 2 * ROWS, HD), BF16),
        (),
        (prompt_keys, prompt_values, resp_keys, resp_values),
        [few, few, pltpu.SemaphoreType.DMA((4,))],
        hbm,
    )
    near_kv = lax.all_gather(kv, "c")
    far_kv = lax.all_gather(lax.ppermute(kv, "yh", swap), "c")
    rows = lax.all_to_all(rows, ("z", "head"), 0, 0, tiled=True)
    packed = pltpu.VMEM((CLASS + BLOCK + 2 * CHUNK, HD), BF16)
    ints = (resp_lengths, resp_order)
    stats = call(
        first_kernel,
        "first_pass",
        shape((NZ, 2 * CHUNKS, CHUNK), F32),
        ints,
        (rows, near_kv, far_kv),
        [
            pltpu.VMEM((2 * CHUNKS, CHUNK), F32),
            packed,
            packed,
            packed,
            pltpu.VMEM((3, 2 * CHUNKS, CHUNK), F32),
        ],
        flops=ROW_FLOPS,
    )
    stats, rows = lax.optimization_barrier((stats, rows))
    rows_y = lax.ppermute(rows, "yh", swap)
    stats = lax.all_to_all(stats, "z", 0, 0, tiled=True)
    mix, qg = call(
        query_kernel,
        "query_pass",
        (shape((2 * CHUNKS, CHUNK), F32), shape((CLASS, HD), BF16)),
        ints,
        (stats, rows, near_kv, far_kv),
        [
            packed,
            packed,
            packed,
            pltpu.VMEM((CLASS, 2 * ROWS), BF16),
            pltpu.VMEM((4 * PROMPT_DEV // KEYS2, HD, KEYS2), BF16),
            pltpu.VMEM((CLASS + BLOCK, HD), F32),
        ],
        flops=ROW_FLOPS,
    )
    terms = lax.all_to_all(
        qg.reshape(NZ * KVH, GROUP, HD), ("z", "head"), 0, 0, tiled=True
    )
    mix, rows_y = lax.optimization_barrier((mix, rows_y))
    mixes = lax.all_gather(mix, "yh")
    acc = pltpu.VMEM((PROMPT_DEV, HD), F32)
    both = pltpu.VMEM((2 * CLASS + BLOCK + 2 * CHUNK, HD), BF16)
    per_chunk = pltpu.VMEM((4 * CHUNKS, CHUNK), F32)

    def key_pass(cross, name, dtype):
        return call(
            functools.partial(key_kernel, cross),
            name,
            shape((2 * PROMPT_DEV + 2 * ROWS, HD), dtype),
            ints,
            (mixes, rows, rows_y, near_kv),
            [both, both, both, per_chunk, per_chunk, acc, acc],
            flops=KEY_FLOPS,
        )

    other = lax.ppermute(key_pass(1, "other_keys", BF16), "c", swap)
    key_grad, value_grad, resp_key_grad, resp_value_grad = call(
        add_kernel,
        "add",
        (
            shape((PROMPT_DEV, HD), BF16),
            shape((PROMPT_DEV, HD), BF16),
            shape((ROWS, HD), BF16),
            shape((ROWS, HD), BF16),
        ),
        (),
        (key_pass(0, "own_keys", F32), other),
    )
    query_grad = call(
        finish_kernel, "finish", shape((1, QH * HD), BF16), (), (terms.reshape(NZ, QH, HD),)
    )
    return query_grad, key_grad, value_grad, resp_key_grad, resp_value_grad


def solution(mesh):
    fine = Mesh(mesh.devices.reshape(2, NZ, 2, KVH), ("yh", "z", "c", "head"))
    ctx = ("yh", "z", "c")
    row = P(ctx + ("head",), None)
    col = P(ctx, "head")
    return jax.shard_map(
        shards,
        mesh=fine,
        in_specs=(row, row, col, col, col, col, P(), P()),
        out_specs=(row, col, col, col, col),
        check_vma=False,
    )
```

```python
import functools
import math

import jax
import jax.numpy as jnp
from jax import lax
from jax.experimental import pallas as pl
from jax.experimental.pallas import tpu as pltpu
from jax.sharding import Mesh
from jax.sharding import PartitionSpec as P

QH = 64
KVH = 8
HD = 128
NRESP = 16
GROUP = QH // KVH
SLOT = 32
NZ = 16
ROWS = 8
BLOCK = ROWS * GROUP
CLASS = NZ * BLOCK
CHUNK = 256
CHUNKS = CLASS // CHUNK
PROMPT_DEV = 768
KEYS1 = 256
KEYS2 = 768
WIDE = 2
SCALE = 1.0 / math.sqrt(HD)
SCALE2 = SCALE * math.log2(math.e)
ROW_FLOPS = 5 * 10**9
KEY_FLOPS = 40 * 10**9
F32 = jnp.float32
BF16 = jnp.bfloat16


def nt(a, b):
    return lax.dot_general(a, b, (((1,), (1,)), ((), ())), preferred_element_type=F32)


def nn(a, b):
    return jnp.dot(a, b, preferred_element_type=F32)


def live_rows(lens_ref, yh, c, z):
    length = lens_ref[yh * (NRESP // 2) + z // 2]
    return jnp.clip(length - ((z % 2) * 2 + c) * ROWS, 0, ROWS)


def chunks_of(lens_ref, yh, c):
    pairs = 0
    for z in range(NZ):
        pairs = pairs + (live_rows(lens_ref, yh, c, z) + 1) // 2
    return (pairs * 16 + CHUNK - 1) // CHUNK


def pack_rows(lens_ref, rows_ref, yh, c, q_ref, g_ref, info_ref):
    in_block = lax.broadcasted_iota(jnp.int32, (BLOCK, HD), 0)
    at = 0
    for z in range(NZ):
        live = live_rows(lens_ref, yh, c, z)
        place = pl.ds(pl.multiple_of(at * 16, 16), BLOCK)
        both = rows_ref[z * ROWS : (z + 1) * ROWS].astype(F32)
        q_ref[place] = both[:, :GROUP].reshape(BLOCK, HD).astype(BF16)
        g = both[:, GROUP:].reshape(BLOCK, HD)
        g_ref[place] = jnp.where(in_block < live * GROUP, g, 0.0).astype(BF16)
        code = (z // 2) * SLOT + ((z % 2) * 2 + c) * ROWS + in_block // GROUP
        info_ref[place] = code.astype(F32).astype(BF16)
        at = at + (live + 1) // 2
    rest = pl.ds(pl.multiple_of(at * 16, 16), CLASS)
    q_ref[rest] = jnp.zeros((CLASS, HD), BF16)
    g_ref[rest] = jnp.zeros((CLASS, HD), BF16)
    info_ref[rest] = jnp.full((CLASS, HD), -SLOT, BF16)
    return (at * 16 + CHUNK - 1) // CHUNK


def unpack_rows(lens_ref, yh, c, acc_ref, out_ref):
    in_block = lax.broadcasted_iota(jnp.int32, (BLOCK, HD), 0)
    at = 0
    for z in range(NZ):
        live = live_rows(lens_ref, yh, c, z)
        block = acc_ref[pl.ds(pl.multiple_of(at * 16, 16), BLOCK)]
        out_ref[z * BLOCK : (z + 1) * BLOCK] = jnp.where(
            in_block < live * GROUP, block, 0.0
        ).astype(BF16)
        at = at + (live + 1) // 2


def key_code(z, c):
    at = lax.broadcasted_iota(jnp.int32, (ROWS, 1), 0)
    return (z // 2) * SLOT + ((z % 2) * 2 + c) * ROWS + at


def row_code(info):
    first = (lax.broadcasted_iota(jnp.int32, (16, HD), 1) == 0).astype(BF16)
    return nt(first, info)[:1].astype(jnp.int32)


def seen_of(rows, keys):
    return (rows >= keys) & (rows < (keys // SLOT + 1) * SLOT)


def stack8(a, b):
    return jnp.concatenate([a.astype(F32), b.astype(F32)], axis=0).astype(BF16)


def send_kernel(q_hbm, g_hbm, rows_ref, q_ref, g_ref, hold_ref, sems):
    copies = [
        pltpu.make_async_copy(q_hbm, q_ref, sems.at[0]),
        pltpu.make_async_copy(g_hbm, g_ref, sems.at[1]),
    ]
    for copy in copies:
        copy.start()
    for copy in copies:
        copy.wait()
    for h in range(QH):
        at = slice(h * HD, (h + 1) * HD)
        hold_ref[h // GROUP, h % GROUP : h % GROUP + 1] = q_ref[:, at].astype(F32)
        hold_ref[h // GROUP, GROUP + h % GROUP : GROUP + h % GROUP + 1] = g_ref[:, at].astype(F32)
    for z in range(NZ):
        rows_ref[z * KVH : (z + 1) * KVH] = hold_ref[...].astype(BF16)


def keys_kernel(
    lengths_ref, order_ref, k_hbm, v_hbm, rk_hbm, rv_hbm, kv_ref, lens_ref, rk_ref, rv_ref, sems
):
    copies = [
        pltpu.make_async_copy(k_hbm, kv_ref.at[:PROMPT_DEV], sems.at[0]),
        pltpu.make_async_copy(v_hbm, kv_ref.at[PROMPT_DEV : 2 * PROMPT_DEV], sems.at[1]),
        pltpu.make_async_copy(rk_hbm, rk_ref, sems.at[2]),
        pltpu.make_async_copy(rv_hbm, rv_ref, sems.at[3]),
    ]
    for copy in copies:
        copy.start()
    for copy in copies:
        copy.wait()
    kv_ref[2 * PROMPT_DEV :] = stack8(rk_ref[...], rv_ref[...])
    for slot in range(NRESP):
        lens_ref[slot] = lengths_ref[order_ref[slot]]


def resp_of(kv_ref):
    a, b = (kv_ref[c, 2 * PROMPT_DEV :].astype(F32) for c in range(2))
    keys = jnp.concatenate([a[:ROWS], b[:ROWS]], axis=0).astype(BF16)
    values = jnp.concatenate([a[ROWS:], b[ROWS:]], axis=0).astype(BF16)
    return keys, values


def lanes_of(ref, first, count):
    return jnp.concatenate([ref[i : i + 1] for i in range(first, first + count)], axis=1)


def key_parts(near_ref, far_ref, step):
    return [
        (ref, c, b) for ref in (near_ref, far_ref) for c in range(2) for b in range(0, PROMPT_DEV, step)
    ]


def first_kernel(
    lens_ref,
    rows_ref,
    near_kv_ref,
    far_kv_ref,
    out_ref,
    packed_ref,
    code_ref,
    stat_ref,
    q_ref,
    g_ref,
    info_ref,
    near_ref,
):
    yh, c, z = lax.axis_index("yh"), lax.axis_index("c"), lax.axis_index("z")
    chunks = pack_rows(lens_ref, rows_ref, yh, c, q_ref, g_ref, info_ref)
    packed_ref[0] = q_ref[:CLASS]
    packed_ref[1] = g_ref[:CLASS]
    stat_ref[...] = jnp.zeros_like(stat_ref)
    resp_k, resp_v = resp_of(near_kv_ref)
    keys = jnp.concatenate([key_code(z, 0), key_code(z, 1)], axis=0)
    codes = row_code(info_ref[:CLASS])
    for i in range(CHUNKS):
        code_ref[i : i + 1] = codes[:, i * CHUNK : (i + 1) * CHUNK]
    seen = seen_of(codes, keys)
    logits = jnp.where(seen, nt(resp_k, q_ref[:CLASS]) * SCALE2, -1e30)
    top = jnp.maximum(jnp.max(logits, axis=0, keepdims=True), -1e29)
    weights = jnp.exp2(logits - top)
    total = jnp.sum(weights, axis=0, keepdims=True)
    inner = jnp.sum(weights * nt(resp_v, g_ref[:CLASS]), axis=0, keepdims=True)
    for i in range(CHUNKS):
        lanes = slice(i * CHUNK, (i + 1) * CHUNK)
        near_ref[0, i : i + 1] = top[:, lanes]
        near_ref[1, i : i + 1] = total[:, lanes]
        near_ref[2, i : i + 1] = inner[:, lanes]

    def chunk(i, _):
        place = pl.ds(pl.multiple_of(i * CHUNK, CHUNK), CHUNK)
        q, g = q_ref[place], g_ref[place]
        top, total, inner = (near_ref[n, pl.ds(i, 1)] for n in range(3))
        for ref, k, b in key_parts(near_kv_ref, far_kv_ref, KEYS1):
            logits = nt(ref[k, b : b + KEYS1], q) * SCALE2
            dprob = nt(ref[k, PROMPT_DEV + b : PROMPT_DEV + b + KEYS1], g)
            now = jnp.maximum(top, jnp.max(logits, axis=0, keepdims=True))
            weights = jnp.exp2(logits - now)
            factor = jnp.exp2(top - now)
            total = total * factor + jnp.sum(weights, axis=0, keepdims=True)
            inner = inner * factor + jnp.sum(weights * dprob, axis=0, keepdims=True)
            top = now
        stat_ref[pl.ds(i, 1)] = top + jnp.log2(total)
        stat_ref[pl.ds(CHUNKS + i, 1)] = inner / total
        return 0

    lax.fori_loop(0, chunks, chunk, 0)
    for n in range(NZ):
        out_ref[n] = stat_ref[...]


def query_kernel(
    lens_ref,
    stats_ref,
    packed_ref,
    code_ref,
    near_kv_ref,
    far_kv_ref,
    keyt_ref,
    mix_ref,
    qg_ref,
    near_ref,
    qacc_ref,
):
    yh, c, z = lax.axis_index("yh"), lax.axis_index("c"), lax.axis_index("z")
    logs = stats_ref[:, :CHUNKS]
    top = jnp.max(logs, axis=0)
    weights = jnp.exp2(logs - top[None])
    total = jnp.sum(weights, axis=0)
    mix_ref[:CHUNKS] = top + jnp.log2(total)
    mix_ref[CHUNKS:] = jnp.sum(weights * stats_ref[:, CHUNKS:], axis=0) / total
    chunks = chunks_of(lens_ref, yh, c)
    resp_k, resp_v = resp_of(near_kv_ref)
    keys = jnp.concatenate([key_code(z, 0), key_code(z, 1)], axis=0)
    seen = seen_of(lanes_of(code_ref, 0, CHUNKS), keys)
    log, delta = lanes_of(mix_ref, 0, CHUNKS), lanes_of(mix_ref, CHUNKS, CHUNKS)
    prob = jnp.exp2(jnp.where(seen, nt(resp_k, packed_ref[0]) * SCALE2 - log, -1e30))
    near_ref[...] = (prob * (nt(resp_v, packed_ref[1]) - delta)).astype(BF16).T

    def chunk(i, _):
        place = pl.ds(pl.multiple_of(i * CHUNK, CHUNK), CHUNK)
        q, g = packed_ref[0, place], packed_ref[1, place]
        log, delta = mix_ref[pl.ds(i, 1)], mix_ref[pl.ds(CHUNKS + i, 1)]
        qgrad = jnp.zeros((HD, CHUNK), F32)
        for n, (ref, core, b) in enumerate(key_parts(near_kv_ref, far_kv_ref, KEYS2)):
            prob = jnp.exp2(nt(ref[core, b : b + KEYS2], q) * SCALE2 - log)
            dprob = nt(ref[core, PROMPT_DEV + b : PROMPT_DEV + b + KEYS2], g)
            qgrad = qgrad + nn(keyt_ref[n], (prob * (dprob - delta)).astype(BF16))
        qacc_ref[place] = (qgrad.T + nn(near_ref[place], resp_k)) * SCALE
        return 0

    lax.fori_loop(0, chunks, chunk, 0)
    unpack_rows(lens_ref, yh, c, qacc_ref, qg_ref)


def turn_kernel(near_kv_ref, far_kv_ref, keyt_ref):
    for n, (ref, core, b) in enumerate(key_parts(near_kv_ref, far_kv_ref, KEYS2)):
        keyt_ref[n] = ref[core, b : b + KEYS2].T


def key_kernel(
    cross,
    lens_ref,
    mix_ref,
    near_ref,
    far_ref,
    code_ref,
    kv_ref,
    out_ref,
    q_ref,
    g_ref,
    log_ref,
    delta_ref,
    kacc_ref,
    vacc_ref,
):
    yh, c, z = lax.axis_index("yh"), lax.axis_index("c"), lax.axis_index("z")
    its_c = 1 - c if cross else c
    kacc_ref[...] = jnp.zeros_like(kacc_ref)
    vacc_ref[...] = jnp.zeros_like(vacc_ref)
    log_ref[...] = jnp.zeros_like(log_ref)
    delta_ref[...] = jnp.zeros_like(delta_ref)
    chunks = 0
    for its_yh, ref in ((yh, near_ref), (1 - yh, far_ref)):
        for i in range(CHUNKS):
            log_ref[pl.ds(chunks + i, 1)] = mix_ref[its_yh, i : i + 1]
            delta_ref[pl.ds(chunks + i, 1)] = mix_ref[its_yh, CHUNKS + i : CHUNKS + i + 1]
        place = pl.ds(pl.multiple_of(chunks * CHUNK, CHUNK), CLASS)
        q_ref[place], g_ref[place] = ref[0], ref[1]
        chunks = chunks + chunks_of(lens_ref, its_yh, c)
    after = pl.ds(pl.multiple_of(chunks * CHUNK, CHUNK), CHUNK)
    q_ref[after] = g_ref[after] = jnp.zeros((CHUNK, HD), BF16)
    resp = kv_ref[its_c, 2 * PROMPT_DEV :]
    none = jnp.zeros((ROWS, HD), F32)
    resp_k = jnp.concatenate([resp[:ROWS].astype(F32), none], axis=0).astype(BF16)
    resp_v = jnp.concatenate([resp[ROWS:].astype(F32), none], axis=0).astype(BF16)
    keys = jnp.concatenate([key_code(z, its_c), jnp.full((ROWS, 1), 1 << 20, jnp.int32)], axis=0)
    seen = seen_of(lanes_of(code_ref, 0, CHUNKS), keys)
    log, delta = lanes_of(mix_ref.at[yh], 0, CHUNKS), lanes_of(mix_ref.at[yh], CHUNKS, CHUNKS)
    q, g = near_ref[0], near_ref[1]
    prob = jnp.exp2(jnp.where(seen, nt(resp_k, q) * SCALE2 - log, -1e30))
    dscore = (prob * (nt(resp_v, g) - delta)).astype(BF16)
    resp_kg = nn(dscore, q)[:ROWS] * SCALE
    resp_vg = nn(prob.astype(BF16), g)[:ROWS]
    out_ref[2 * PROMPT_DEV :] = jnp.concatenate([resp_kg, resp_vg], axis=0).astype(out_ref.dtype)

    def step(n, _):
        place = pl.ds(pl.multiple_of(n * WIDE * CHUNK, CHUNK), WIDE * CHUNK)
        q, g = q_ref[place], g_ref[place]
        log = jnp.concatenate([log_ref[pl.ds(WIDE * n + i, 1)] for i in range(WIDE)], axis=1)
        delta = jnp.concatenate([delta_ref[pl.ds(WIDE * n + i, 1)] for i in range(WIDE)], axis=1)
        prob = jnp.exp2(nt(kv_ref[its_c, :PROMPT_DEV], q) * SCALE2 - log)
        dprob = nt(kv_ref[its_c, PROMPT_DEV : 2 * PROMPT_DEV], g)
        dscore = (prob * (dprob - delta)).astype(BF16)
        kacc_ref[...] += nn(dscore, q)
        vacc_ref[...] += nn(prob.astype(BF16), g)
        return 0

    lax.fori_loop(0, (chunks + WIDE - 1) // WIDE, step, 0)
    out_ref[:PROMPT_DEV] = (kacc_ref[...] * SCALE).astype(out_ref.dtype)
    out_ref[PROMPT_DEV : 2 * PROMPT_DEV] = vacc_ref[...].astype(out_ref.dtype)


def finish_kernel(
    terms_ref, mine_ref, other_ref, qg_ref, kg_ref, vg_ref, rkg_ref, rvg_ref
):
    total = jnp.sum(terms_ref[...].astype(F32), axis=0)
    for h in range(QH):
        qg_ref[:, h * HD : (h + 1) * HD] = total[h : h + 1].astype(BF16)
    resp = 2 * PROMPT_DEV
    kg_ref[...] = (mine_ref[:PROMPT_DEV] + other_ref[:PROMPT_DEV].astype(F32)).astype(BF16)
    vg_ref[...] = (mine_ref[PROMPT_DEV:resp] + other_ref[PROMPT_DEV:resp].astype(F32)).astype(BF16)
    rest = mine_ref[resp:] + other_ref[resp:].astype(F32)
    rkg_ref[...] = rest[:ROWS].astype(BF16)
    rvg_ref[...] = rest[ROWS:].astype(BF16)


def shards(
    queries, out_grad, resp_keys, resp_values, prompt_keys, prompt_values, resp_lengths, resp_order
):
    vmem = pl.BlockSpec(memory_space=pltpu.VMEM)
    smem = pl.BlockSpec(memory_space=pltpu.SMEM)
    hbm = pl.BlockSpec(memory_space=pltpu.HBM)
    swap = [(0, 1), (1, 0)]
    shape = jax.ShapeDtypeStruct

    def call(
        kernel, name, out_shape, ints, arrays, scratch=(), space=vmem, flops=0, out=None, limit=32
    ):
        cost = pl.CostEstimate(flops=flops, bytes_accessed=0, transcendentals=0) if flops else None
        return pl.pallas_call(
            kernel,
            out_shape=out_shape,
            in_specs=[smem] * len(ints) + [space] * len(arrays),
            out_specs=out or jax.tree.map(lambda _: vmem, out_shape),
            scratch_shapes=list(scratch),
            compiler_params=pltpu.CompilerParams(vmem_limit_bytes=limit * 1024 * 1024),
            cost_estimate=cost,
            name=name,
        )(*ints, *arrays)

    whole = pltpu.VMEM((1, QH * HD), BF16)
    rows = call(
        send_kernel,
        "send",
        shape((NZ * KVH, 2 * GROUP, HD), BF16),
        (),
        (queries, out_grad),
        [whole, whole, pltpu.VMEM((KVH, 2 * GROUP, HD), F32), pltpu.SemaphoreType.DMA((2,))],
        hbm,
        limit=60,
    )
    few = pltpu.VMEM((ROWS, HD), BF16)
    kv, lens = call(
        keys_kernel,
        "keys",
        (shape((2 * PROMPT_DEV + 2 * ROWS, HD), BF16), shape((NRESP,), jnp.int32)),
        (resp_lengths, resp_order),
        (prompt_keys, prompt_values, resp_keys, resp_values),
        [few, few, pltpu.SemaphoreType.DMA((4,))],
        hbm,
        out=(vmem, smem),
    )
    near_kv = lax.all_gather(kv, "c")
    far_kv = lax.all_gather(lax.ppermute(kv, "yh", swap), "c")
    rows = lax.all_to_all(rows, ("z", "head"), 0, 0, tiled=True)
    keyt = call(
        turn_kernel,
        "turn",
        shape((4 * PROMPT_DEV // KEYS2, HD, KEYS2), BF16),
        (),
        (near_kv, far_kv),
    )
    hold = pltpu.VMEM((2 * CLASS + BLOCK, HD), BF16)
    ints = (lens,)
    lanes = shape((2 * CHUNKS, CHUNK), F32)
    stats, packed, code = call(
        first_kernel,
        "first_pass",
        (
            shape((NZ, 2 * CHUNKS, CHUNK), F32),
            shape((2, CLASS, HD), BF16),
            shape((2 * CHUNKS, CHUNK), jnp.int32),
        ),
        ints,
        (rows, near_kv, far_kv),
        [
            pltpu.VMEM((2 * CHUNKS, CHUNK), F32),
            hold,
            hold,
            hold,
            pltpu.VMEM((3, 2 * CHUNKS, CHUNK), F32),
        ],
        flops=ROW_FLOPS,
    )
    far_packed = lax.ppermute(packed, "yh", swap)
    stats = lax.all_to_all(stats, "z", 0, 0, tiled=True)
    mix, qg = call(
        query_kernel,
        "query_pass",
        (lanes, shape((CLASS, HD), BF16)),
        ints,
        (stats, packed, code, near_kv, far_kv, keyt),
        [pltpu.VMEM((CLASS, 2 * ROWS), BF16), pltpu.VMEM((CLASS + BLOCK, HD), F32)],
        flops=ROW_FLOPS,
    )
    terms = lax.all_to_all(
        qg.reshape(NZ * KVH, GROUP, HD), ("z", "head"), 0, 0, tiled=True
    )
    mix, far_packed = lax.optimization_barrier((mix, far_packed))
    mixes = lax.all_gather(mix, "yh")
    acc = pltpu.VMEM((PROMPT_DEV, HD), F32)
    both = pltpu.VMEM((2 * CLASS + CHUNK, HD), BF16)
    per_chunk = pltpu.VMEM((4 * CHUNKS, CHUNK), F32)

    def key_pass(cross, name, dtype):
        return call(
            functools.partial(key_kernel, cross),
            name,
            shape((2 * PROMPT_DEV + 2 * ROWS, HD), dtype),
            ints,
            (mixes, packed, far_packed, code, near_kv),
            [both, both, per_chunk, per_chunk, acc, acc],
            flops=KEY_FLOPS,
        )

    other = lax.ppermute(key_pass(1, "other_keys", BF16), "c", swap)
    return call(
        finish_kernel,
        "finish",
        (
            shape((1, QH * HD), BF16),
            shape((PROMPT_DEV, HD), BF16),
            shape((PROMPT_DEV, HD), BF16),
            shape((ROWS, HD), BF16),
            shape((ROWS, HD), BF16),
        ),
        (),
        (terms.reshape(NZ, QH, HD), key_pass(0, "own_keys", F32), other),
    )


def solution(mesh):
    fine = Mesh(mesh.devices.reshape(2, NZ, 2, KVH), ("yh", "z", "c", "head"))
    ctx = ("yh", "z", "c")
    row = P(ctx + ("head",), None)
    col = P(ctx, "head")
    return jax.shard_map(
        shards,
        mesh=fine,
        in_specs=(row, row, col, col, col, col, P(), P()),
        out_specs=(row, col, col, col, col),
        check_vma=False,
    )
```
